32 devices in a mesh: row: 8 (over y, x, core), col: 4 (over z).
Axes of the slice: x: 2, y: 2, z: 4, core: 2. Of those that a mesh axis runs over, the one named last changes fastest.
Arguments:
- left_panels: float32 [3, 64, 65536], P(None, 'col', 'row'), may hold values from -0.0234375 to 0.0234375
- right_panels: float32 [3, 65536, 512], P(None, 'row', 'col'), may hold values from -6 to 6
- window_tiles: float32 [3, 64, 512], P(None, 'row', 'col'), may hold values from -6 to 6
Outputs:
- updated: float32 [3, 64, 512], P(None, 'row', 'col')
The draws below stay inside these ranges and needn't reach their ends.
All inputs are finite; a program needn't handle non-finite values.
Results may differ from the reference program's by a relative error of at most 0.00005.
Values sent between devices are 32-bit elements; how exact they have to be, the bound alone decides.
No kernel may reach another device: no remote copies, remote signals or barrier semaphores. Data moves between devices by JAX's collectives and lax.ppermute only.
A program may use at most 64 MiB of HBM per device.

```python
import jax
import jax.numpy as jnp
from jax import lax

ORDER = 65536
ROWS = 64
COLS = 512


def block_scale(key, extent, shards, smallest, high):
    loudness, own = 1.0, jax.random.fold_in(key, 6)
    for dim, shards_of in shards:
        heights = jnp.exp(jax.random.uniform(jax.random.fold_in(own, dim), (shards_of,), jnp.float32, smallest / len(shards), high / len(shards)))
        loudness = loudness * jnp.repeat(heights, extent[dim] // shards_of).reshape([-1 if axis == dim else 1 for axis in range(len(extent))])
    return loudness


def bell_draw(own_key, shape, scale, bound, cuts=(), dtype=jnp.bfloat16):
    factor_of = block_scale(own_key, shape, cuts, -0.22, 0.18) if cuts else 1.0
    entries = jax.random.normal(own_key, shape, jnp.float32) * scale * factor_of
    return jnp.minimum(jnp.maximum(entries, -bound), bound).astype(dtype)


def setup_inputs(seed: int = 0) -> dict:
    keys = jax.random.split(jax.random.key(seed), 4)
    return {
        "left_panels": bell_draw(keys[0], (3, ROWS, ORDER), ORDER ** -0.5, 0.0234375, ((1, 4), (2, 8)), jnp.float32),
        "right_panels": bell_draw(keys[1], (3, ORDER, COLS), 1.0, 6.0, ((1, 8), (2, 4)), jnp.float32),
        "window_tiles": bell_draw(keys[2], (3, ROWS, COLS), 1.0, 6.0, ((1, 8), (2, 4)), jnp.float32),
    }


def product(left_part, right_part):
    return jnp.dot(left_part, right_part, precision=lax.Precision.HIGHEST, preferred_element_type=jnp.float32)


def reference(left_panels, right_panels, window_tiles):
    square = product(left_panels[0], right_panels[0])
    first = product(left_panels[0], right_panels[1]) + product(left_panels[1], right_panels[0])
    second = product(left_panels[0], right_panels[2]) + product(left_panels[1], right_panels[1]) + product(left_panels[2], right_panels[0])
    return jnp.stack([2.0 * window_tiles[0] - square, 2.0 * window_tiles[1] - first, 2.0 * window_tiles[2] - second])
```

```python
import functools

import jax
import jax.numpy as jnp
from jax import lax
from jax.experimental import pallas as pl
from jax.experimental.pallas import tpu as pltpu
from jax.sharding import PartitionSpec as P

ORDERS = 3
VMEM_LIMIT = 48 * 1024 * 1024


def halves(values):
    high = values.astype(jnp.bfloat16)
    return high, (values - high.astype(jnp.float32)).astype(jnp.bfloat16)


def products_kernel(layout, steps, *refs):
    count = sum(sum(sources) for sources in layout)
    left_refs, right_ref, out_ref = refs[:count], refs[count], refs[count + 1]
    totals = refs[count + 2 :]
    sources_of = [len(sources) for sources in layout]
    step = pl.program_id(0)

    rows, place = [], 0
    for sources in layout:
        for arrays in sources:
            piece = left_refs[place][...]
            for extra in range(1, arrays):
                piece = piece + left_refs[place + extra][...]
            place += arrays
            rows.extend(halves(piece))
    height = rows[0].shape[0]
    stacked = jnp.concatenate(rows, axis=0)
    for order, parts in enumerate(totals):
        high, low = halves(right_ref[order])
        used = 2 * height * sum(sources_of[: ORDERS - order])
        parts[step] = jnp.dot(
            stacked[:used], jnp.concatenate([high, low], axis=1), preferred_element_type=jnp.float32
        )

    @pl.when(step == steps - 1)
    def _():
        width = right_ref.shape[2]
        sums = [jnp.sum(parts[...], axis=0) for parts in totals]
        for source in range(max(sources_of)):
            for out_order in range(ORDERS):
                value = jnp.zeros((height, width), jnp.float32)
                first_row = 0
                for left_order in range(ORDERS):
                    right_order = out_order - left_order
                    if 0 <= right_order < len(totals) and source < sources_of[left_order]:
                        top = (first_row + source) * 2 * height
                        block = sums[right_order][top : top + 2 * height]
                        block = block[:height] + block[height:]
                        value = value + (block[:, :width] + block[:, width:])
                    first_row += sources_of[left_order]
                out_ref[source, out_order] = value


def products(lefts, right, start=0, extent=None, tile=1024):
    height = next(arrays[0].shape[0] for sources in lefts for arrays in sources)
    extent = next(arrays[0].shape[1] for sources in lefts for arrays in sources) if extent is None else extent
    width = right.shape[2]
    tile = min(tile, extent)
    steps = extent // tile
    layout = [[len(arrays) for arrays in sources] for sources in lefts]
    flat = [array for sources in lefts for arrays in sources for array in arrays]
    sources_of = [len(sources) for sources in lefts]
    lowest = min(a for a in range(ORDERS) if sources_of[a])
    right_orders = min(ORDERS - lowest, right.shape[0])
    first_block = start // tile
    multiplies = sum(
        2 * height * sum(sources_of[: ORDERS - order]) * extent * 2 * width for order in range(right_orders)
    )
    return pl.pallas_call(
        functools.partial(products_kernel, layout, steps),
        grid=(steps,),
        in_specs=[pl.BlockSpec((height, tile), lambda k: (0, k))] * len(flat)
        + [pl.BlockSpec((right_orders, tile, width), lambda k: (0, k + first_block, 0))],
        out_specs=pl.BlockSpec((max(sources_of), ORDERS, height, width), lambda k: (0, 0, 0, 0)),
        out_shape=jax.ShapeDtypeStruct((max(sources_of), ORDERS, height, width), jnp.float32),
        scratch_shapes=[
            pltpu.VMEM((steps, 2 * height * sum(sources_of[: ORDERS - order]), 2 * width), jnp.float32)
            for order in range(right_orders)
        ],
        compiler_params=pltpu.CompilerParams(vmem_limit_bytes=VMEM_LIMIT),
        cost_estimate=pl.CostEstimate(
            flops=2 * multiplies,
            bytes_accessed=4 * (len(flat) * height * extent + right_orders * extent * width),
            transcendentals=0,
        ),
    )(*flat, right)


def sum_over_row(blocks, row_size):
    if row_size != 8:
        return lax.psum_scatter(blocks, "row", scatter_dimension=0, tiled=True)[0]
    me = lax.axis_index("row")
    pairs = blocks.reshape((4, 2) + blocks.shape[1:])
    core, chip = me % 2, me // 2
    keep = lax.dynamic_index_in_dim(pairs, core, 1, False)
    give = lax.dynamic_index_in_dim(pairs, 1 - core, 1, False)
    mine = keep + lax.ppermute(give, "row", [(i, i ^ 1) for i in range(8)])
    total = lax.dynamic_index_in_dim(mine, chip, 0, False)
    for offset in (1, 2, 3):
        block = lax.dynamic_index_in_dim(mine, chip ^ offset, 0, False)
        total = total + lax.ppermute(block, "row", [(i, i ^ (2 * offset)) for i in range(8)])
    return total


def line_of_four(left, right):
    place = lax.axis_index("col")
    swap = [(0, 1), (1, 0), (2, 3), (3, 2)]
    middle = [(1, 2), (2, 1)]
    outward = [(1, 0), (2, 3)]
    send = lambda array, pairs: lax.ppermute(array, "col", pairs)
    own = [left[order] for order in range(ORDERS)]
    near = [send(piece, swap) for piece in own]
    across = [send(piece, middle) for piece in own]
    across_out = [send(piece, outward) for piece in across]
    far = [send(piece, middle) for piece in near]
    far_out = [send(piece, outward) for piece in far]
    first = products([[(own[a],), (near[a],)] for a in range(ORDERS)], right)
    second = products([[(across[a], across_out[a])] for a in range(ORDERS)], right)
    third = products([[(far[a], far_out[a])] for a in range(ORDERS)], right)
    shards = jnp.stack([first[0], first[1], second[0], third[0]])
    slots = lambda *shards_at: functools.reduce(lambda rest, at: jnp.where(place == at[0], at[1], rest), enumerate(shards_at), 0)
    where_is = (slots(0, 1, 3, 3), slots(1, 0, 2, 2), slots(2, 2, 0, 1), slots(3, 3, 1, 0))
    return jnp.stack([lax.dynamic_index_in_dim(shards, slot, 0, False) for slot in where_is])


def on_device(cols, rows, left_panels, right_panels, window_tiles):
    height, width = window_tiles.shape[1:]
    if cols == 4:
        shards = line_of_four(left_panels, right_panels)
    else:
        gathered = lax.all_gather(left_panels, "col", axis=1, tiled=True)
        shards = products([[(gathered[a],)] for a in range(ORDERS)], right_panels)
    blocks = shards.reshape(-1, ORDERS, shards.shape[2] // height, height, width)
    blocks = jnp.swapaxes(blocks, 1, 2).reshape(rows, ORDERS, height, width)
    return 2.0 * window_tiles - sum_over_row(blocks, rows)


def solution(mesh):
    return jax.shard_map(
        functools.partial(on_device, mesh.shape["col"], mesh.shape["row"]),
        mesh=mesh,
        in_specs=(P(None, "col", "row"), P(None, "row", "col"), P(None, "row", "col")),
        out_specs=P(None, "row", "col"),
        check_vma=False,
    )
```

```python
import functools

import jax
import jax.numpy as jnp
from jax import lax
from jax.experimental import pallas as pl
from jax.experimental.pallas import tpu as pltpu
from jax.sharding import PartitionSpec as P

ORDERS = 3
LANES, SUBLANES = 128, 8
TILE = 1024
VMEM_LIMIT = 12 * 1024 * 1024


def halves(values):
    high = values.astype(jnp.bfloat16)
    return high, (values - high.astype(jnp.float32)).astype(jnp.bfloat16)


def blocked(left):
    height, extent = left.shape
    return left.reshape(height // SUBLANES, SUBLANES, extent // LANES, LANES).transpose(0, 2, 1, 3)


def unblocked(blocks):
    return jnp.concatenate(
        [jnp.concatenate([blocks[a, c] for c in range(blocks.shape[1])], axis=1) for a in range(blocks.shape[0])], axis=0
    )


def products_kernel(layout, steps, side_ref, *refs):
    count = sum(len(terms) for sources in layout for terms in sources)
    left_refs, right_ref, out_ref = refs[:count], refs[count], refs[count + 1]
    totals = refs[count + 2 :]
    sources_of = [len(sources) for sources in layout]
    step = pl.program_id(0)

    rows, place = [], 0
    for sources in layout:
        for terms in sources:
            piece = None
            for first, tiles, side in terms:
                term = unblocked(left_refs[place][...])
                counts = None
                if tiles < steps:
                    counts = (step >= first) & (step < first + tiles)
                if side is not None:
                    here = side_ref[0] == side
                    counts = here if counts is None else counts & here
                if counts is not None:
                    term = jnp.where(counts, term, 0.0)
                piece = term if piece is None else piece + term
                place += 1
            rows.extend(halves(piece))
    height = rows[0].shape[0]
    stacked = jnp.concatenate(rows, axis=0)
    for order, parts in enumerate(totals):
        high, low = halves(right_ref[order])
        used = 2 * height * sum(sources_of[: ORDERS - order])
        parts[step] = jnp.dot(
            stacked[:used], jnp.concatenate([high, low], axis=1), preferred_element_type=jnp.float32
        )

    @pl.when(step == steps - 1)
    def _():
        width = right_ref.shape[2]
        sums = [jnp.sum(parts[...], axis=0) for parts in totals]
        for source in range(max(sources_of)):
            for out_order in range(ORDERS):
                value = jnp.zeros((height, width), jnp.float32)
                first_row = 0
                for left_order in range(ORDERS):
                    right_order = out_order - left_order
                    if 0 <= right_order < len(totals) and source < sources_of[left_order]:
                        top = (first_row + source) * 2 * height
                        block = sums[right_order][top : top + 2 * height]
                        block = block[:height] + block[height:]
                        value = value + (block[:, :width] + block[:, width:])
                    first_row += sources_of[left_order]
                out_ref[source, out_order] = value


def products(lefts, right, extent, side):
    flat = [term for sources in lefts for terms in sources for term in terms]
    high_blocks = flat[0][1].shape[0]
    height = high_blocks * SUBLANES
    width = right.shape[2]
    tile = min(TILE, extent)
    steps = extent // tile
    tiles_of = lambda array: array.shape[1] * LANES // tile
    layout = [
        [[(first // tile, tiles_of(array), on) for first, array, on in terms] for terms in sources] for sources in lefts
    ]
    sources_of = [len(sources) for sources in lefts]
    right_orders = min(ORDERS - min(a for a in range(ORDERS) if sources_of[a]), right.shape[0])
    rows_of = [2 * height * sum(sources_of[: ORDERS - order]) for order in range(right_orders)]

    def left_spec(first, array, on):
        first, last = first // tile, tiles_of(array) - 1
        return pl.BlockSpec(
            (high_blocks, tile // LANES, SUBLANES, LANES), lambda k: (0, jnp.clip(k - first, 0, last), 0, 0)
        )

    return pl.pallas_call(
        functools.partial(products_kernel, layout, steps),
        grid=(steps,),
        in_specs=[pl.BlockSpec(memory_space=pltpu.SMEM)]
        + [left_spec(*term) for term in flat]
        + [pl.BlockSpec((right_orders, tile, width), lambda k: (0, k, 0))],
        out_specs=pl.BlockSpec((max(sources_of), ORDERS, height, width), lambda k: (0, 0, 0, 0)),
        out_shape=jax.ShapeDtypeStruct((max(sources_of), ORDERS, height, width), jnp.float32),
        scratch_shapes=[pltpu.VMEM((steps, rows, 2 * width), jnp.float32) for rows in rows_of],
        compiler_params=pltpu.CompilerParams(vmem_limit_bytes=VMEM_LIMIT),
        cost_estimate=pl.CostEstimate(
            flops=4 * sum(rows_of) * extent * width,
            bytes_accessed=4 * (sum(term[1].size for term in flat) + right_orders * extent * width),
            transcendentals=0,
        ),
    )(side, *[term[1] for term in flat], right)


def sum_over_row(blocks, row_size):
    if row_size != 8:
        return lax.psum_scatter(blocks, "row", scatter_dimension=0, tiled=True)[0]
    me = lax.axis_index("row")
    pairs = blocks.reshape((4, 2) + blocks.shape[1:])
    core, chip = me % 2, me // 2
    keep = lax.dynamic_index_in_dim(pairs, core, 1, False)
    give = lax.dynamic_index_in_dim(pairs, 1 - core, 1, False)
    mine = keep + lax.ppermute(give, "row", [(i, i ^ 1) for i in range(8)])
    total = lax.dynamic_index_in_dim(mine, chip, 0, False)
    for offset in (1, 2, 3):
        block = lax.dynamic_index_in_dim(mine, chip ^ offset, 0, False)
        total = total + lax.ppermute(block, "row", [(i, i ^ (2 * offset)) for i in range(8)])
    return total


def after(array, *earlier):
    return lax.optimization_barrier((array, *earlier))[0]


END, INNER = 1, 0


def line_of_four(left, right):
    place = lax.axis_index("col")
    at_end = (place == 0) | (place == 3)
    side = at_end.astype(jnp.int32).reshape(1)
    pairs = lambda array, *earlier: lax.ppermute(after(array, *earlier), "col", [(0, 1), (1, 0), (2, 3), (3, 2)])
    middle = lambda array, *earlier: lax.ppermute(after(array, *earlier), "col", [(1, 2), (2, 1)])
    outward = lambda array: lax.ppermute(array, "col", [(1, 0), (2, 3)])
    extent = left.shape[2]
    half = extent // 2
    own0, own1, own2, own3 = blocked(left[0]), blocked(left[1]), blocked(left[2, :, :half]), blocked(left[2, :, half:])
    depth = own0.size // right.shape[2]
    chunk = lambda i: right[0, half + i * depth : half + (i + 1) * depth].reshape(own0.shape)
    chunks = half // depth

    near0 = pairs(own0)
    across0 = middle(own0)
    near1 = pairs(own1)
    across1 = middle(own1)
    near2 = pairs(own2, near0)
    across2 = middle(own2, across0)
    out0 = pairs(jnp.where(at_end, chunk(0), across0), near1)
    across3 = middle(own3, across1)
    out1 = pairs(jnp.where(at_end, chunk(1), across1), near2)
    far0 = middle(near0, across2)
    out2 = pairs(jnp.where(at_end, own3, across2), out0)
    far1 = middle(near1, across3)
    far2 = middle(near2, far0)
    far_out0 = pairs(jnp.where(at_end, chunk(2), far0), out1)
    far3 = middle(out2, far1)
    far_out1 = pairs(jnp.where(at_end, chunk(3), far1), out2)
    far_out2 = pairs(far2, far_out0)

    full = lambda array: (0, array, None)
    at_ends = lambda array: (0, array, END)
    first = products(
        [
            [[full(own0)], [full(near0)]],
            [[full(own1)], [full(near1)]],
            [[full(own2), (half, own3, None)], [full(near2)]],
        ],
        right,
        extent,
        side,
    )
    second = products(
        [
            [[full(across0), at_ends(out0)]],
            [[full(across1), at_ends(out1)]],
            [[full(across2), at_ends(out2), (half, across3, None)]],
        ],
        right,
        extent,
        side,
    )
    third = products(
        [[[full(far0), at_ends(far_out0)]], [], [[(half, far3, None)], [(half, out2, INNER)]]], right, extent, side
    )
    rest = lambda array, i: array[:, i * depth // LANES : (i + 1) * depth // LANES]
    for_end = [
        products(
            [[], [], [[full(rest(piece, i))] for piece in (own3, across3, far3)]],
            panel.reshape(1, depth, right.shape[2]),
            depth,
            side,
        )[:, 2]
        for i, panel in enumerate((out0, out1, far_out0, far_out1))
    ]
    from_neighbour = outward(functools.reduce(jnp.add, for_end))
    fourth = products([[], [[full(far1), at_ends(far_out1)]], []], right, extent, side)
    fifth = products([[], [], [[full(far2), at_ends(far_out2)]]], right, half, side)

    shards = jnp.stack([first[0], first[1], second[0], third[0] + fourth[0] + fifth[0]])
    shards = shards.at[1, 2].add(third[1, 2])
    shards = shards.at[1:, 2].add(from_neighbour)
    slots = lambda *at: functools.reduce(lambda rest, i: jnp.where(place == i, at[i], rest), range(3), at[3])
    where_is = (slots(0, 1, 3, 3), slots(1, 0, 2, 2), slots(2, 2, 0, 1), slots(3, 3, 1, 0))
    return jnp.stack([lax.dynamic_index_in_dim(shards, slot, 0, False) for slot in where_is])


def on_device(cols, rows, left_panels, right_panels, window_tiles):
    height, width = window_tiles.shape[1:]
    if cols == 4:
        shards = line_of_four(left_panels, right_panels)
    else:
        gathered = lax.all_gather(left_panels, "col", axis=1, tiled=True)
        lefts = [[[(0, blocked(gathered[a]), None)]] for a in range(ORDERS)]
        shards = products(lefts, right_panels, right_panels.shape[1], jnp.zeros((1,), jnp.int32))
    blocks = shards.reshape(-1, ORDERS, shards.shape[2] // height, height, width)
    blocks = jnp.swapaxes(blocks, 1, 2).reshape(rows, ORDERS, height, width)
    return 2.0 * window_tiles - sum_over_row(blocks, rows)


def solution(mesh):
    return jax.shard_map(
        functools.partial(on_device, mesh.shape["col"], mesh.shape["row"]),
        mesh=mesh,
        in_specs=(P(None, "col", "row"), P(None, "row", "col"), P(None, "row", "col")),
        out_specs=P(None, "row", "col"),
        check_vma=False,
    )
```

```python
import functools

import jax
import jax.numpy as jnp
from jax import lax
from jax.experimental import pallas as pl
from jax.experimental.pallas import tpu as pltpu
from jax.sharding import PartitionSpec as P

ORDERS = 3
LANES, SUBLANES = 128, 8
TILE = 1024
VMEM_LIMIT = 48 * 1024 * 1024


def halves(values):
    high = values.astype(jnp.bfloat16)
    return high, (values - high.astype(jnp.float32)).astype(jnp.bfloat16)


def blocked(left):
    height, extent = left.shape
    return left.reshape(height // SUBLANES, SUBLANES, extent // LANES, LANES).transpose(0, 2, 1, 3)


def unblocked(blocks):
    return jnp.concatenate(
        [jnp.concatenate([blocks[a, c] for c in range(blocks.shape[1])], axis=1) for a in range(blocks.shape[0])], axis=0
    )


def products_kernel(layout, steps, orders, keep, side_ref, *refs):
    count = sum(len(terms) for sources in layout for terms in sources)
    left_refs, right_ref, out_ref = refs[:count], refs[count], refs[count + 1]
    kept_ref = refs[count + 2] if keep else None
    scratch = refs[count + 2 + bool(keep) :]
    totals, held = scratch[:orders], scratch[orders:]
    sources_of = [len(sources) for sources in layout]
    tile = right_ref.shape[1] // steps if not held else held[0].shape[1] // steps
    columns = tile // LANES

    def arrival(step):
        rows = pl.ds(step * tile, tile)
        return pltpu.make_async_copy(right_ref.at[:orders, rows], held[0].at[:, rows], held[1].at[step])

    def kept():
        return pltpu.make_async_copy(right_ref.at[:1, :keep], kept_ref, held[1].at[steps])

    if held:
        for step in range(steps):
            arrival(step).start()
        if keep:
            kept().start()
    panels = held[0] if held else right_ref

    @pl.loop(0, steps)
    def _(step):
        if held:
            arrival(step).wait()
        rows, place = [], 0
        for sources in layout:
            for terms in sources:
                piece = None
                for first, tiles, skip, side in terms:
                    at = skip + (jnp.clip(step - first, 0, tiles - 1) if tiles < steps else step)
                    term = unblocked(left_refs[place][:, pl.ds(at * columns, columns)])
                    counts = None
                    if tiles < steps:
                        counts = (step >= first) & (step < first + tiles)
                    if side is not None:
                        here = side_ref[0] == side
                        counts = here if counts is None else counts & here
                    if counts is not None:
                        term = jnp.where(counts, term, 0.0)
                    piece = term if piece is None else piece + term
                    place += 1
                rows.extend(halves(piece))
        stacked = jnp.concatenate(rows, axis=0)
        height = rows[0].shape[0]
        for order, parts in enumerate(totals):
            panel = jnp.concatenate(halves(panels[order, pl.ds(step * tile, tile), :]), axis=1)
            used = 2 * height * sum(sources_of[: ORDERS - order])
            parts[step] = jnp.dot(stacked[:used], panel, preferred_element_type=jnp.float32)

    if keep:
        kept().wait()
    height, width = out_ref.shape[2:]
    sums = [jnp.sum(parts[...], axis=0) for parts in totals]
    for source in range(max(sources_of)):
        for out_order in range(ORDERS):
            value = jnp.zeros((height, width), jnp.float32)
            first_row = 0
            for left_order in range(ORDERS):
                right_order = out_order - left_order
                if 0 <= right_order < len(totals) and source < sources_of[left_order]:
                    top = (first_row + source) * 2 * height
                    block = sums[right_order][top : top + 2 * height]
                    block = block[:height] + block[height:]
                    value = value + (block[:, :width] + block[:, width:])
                first_row += sources_of[left_order]
            out_ref[source, out_order] = value


def products(lefts, right, extent, side, resident=False, keep=0):
    flat = [term for sources in lefts for terms in sources for term in terms]
    height = flat[0][1].shape[0] * SUBLANES
    width = right.shape[2]
    tile = min(TILE, extent)
    steps = extent // tile
    tiles_of = lambda array, part: (extent if part is not None else array.shape[1] * LANES) // tile
    layout = [
        [
            [(first // tile, tiles_of(array, part), (part or 0) * steps, on) for first, array, on, part in terms]
            for terms in sources
        ]
        for sources in lefts
    ]
    sources_of = [len(sources) for sources in lefts]
    orders = min(ORDERS - min(a for a in range(ORDERS) if sources_of[a]), right.shape[0])
    rows_of = [2 * height * sum(sources_of[: ORDERS - order]) for order in range(orders)]
    in_vmem = pl.BlockSpec(memory_space=pltpu.VMEM)
    held = [] if resident else [
        pltpu.VMEM((orders, extent, width), jnp.float32),
        pltpu.SemaphoreType.DMA((steps + bool(keep),)),
    ]
    out = jax.ShapeDtypeStruct((max(sources_of), ORDERS, height, width), jnp.float32)
    kept = jax.ShapeDtypeStruct((1, keep, width), jnp.float32)
    return pl.pallas_call(
        functools.partial(products_kernel, layout, steps, orders, keep),
        in_specs=[pl.BlockSpec(memory_space=pltpu.SMEM)]
        + [in_vmem] * len(flat)
        + [in_vmem if resident else pl.BlockSpec(memory_space=pltpu.HBM)],
        out_specs=(in_vmem, in_vmem) if keep else in_vmem,
        out_shape=(out, kept) if keep else out,
        scratch_shapes=[pltpu.VMEM((steps, rows, 2 * width), jnp.float32) for rows in rows_of] + held,
        compiler_params=pltpu.CompilerParams(vmem_limit_bytes=VMEM_LIMIT),
        cost_estimate=pl.CostEstimate(
            flops=4 * sum(rows_of) * extent * width,
            bytes_accessed=4 * (sum(term[1].size for term in flat) + orders * extent * width),
            transcendentals=0,
        ),
    )(side, *[term[1] for term in flat], right)


def sum_over_row(blocks, row_size):
    if row_size != 8:
        return lax.psum_scatter(blocks, "row", scatter_dimension=0, tiled=True)[0]
    me = lax.axis_index("row")
    pairs = blocks.reshape((4, 2) + blocks.shape[1:])
    core, chip = me % 2, me // 2
    keep = lax.dynamic_index_in_dim(pairs, core, 1, False)
    give = lax.dynamic_index_in_dim(pairs, 1 - core, 1, False)
    mine = keep + lax.ppermute(give, "row", [(i, i ^ 1) for i in range(8)])
    total = lax.dynamic_index_in_dim(mine, chip, 0, False)
    for offset in (1, 2, 3):
        block = lax.dynamic_index_in_dim(mine, chip ^ offset, 0, False)
        total = total + lax.ppermute(block, "row", [(i, i ^ (2 * offset)) for i in range(8)])
    return total


def after(array, *earlier):
    return lax.optimization_barrier((array, *earlier))[0]


END, INNER = 1, 0


def line_of_four(left, right):
    place = lax.axis_index("col")
    at_end = (place == 0) | (place == 3)
    side = at_end.astype(jnp.int32).reshape(1)
    pairs = lambda array, *earlier: lax.ppermute(after(array, *earlier), "col", [(0, 1), (1, 0), (2, 3), (3, 2)])
    middle = lambda array, *earlier: lax.ppermute(after(array, *earlier), "col", [(1, 2), (2, 1)])
    outward = lambda array: lax.ppermute(array, "col", [(1, 0), (2, 3)])
    extent = left.shape[2]
    half = extent // 2
    own0, own1 = blocked(left[0]), blocked(left[1])
    left2 = after(left, own0, own1)[2]
    own2, own3 = blocked(left2[:, :half]), blocked(left2[:, half:])
    width = right.shape[2]
    depth = own0.size // width
    chunk = lambda i: right[0, half + i * depth : half + (i + 1) * depth].reshape(own0.shape)
    full = lambda array: (0, array, None, None)
    at_ends = lambda array: (0, array, END, None)
    upper = lambda array, on: (half, array, on, None)

    near0 = pairs(own0)
    across0 = middle(own0)
    near1 = pairs(own1)
    across1 = middle(own1)
    near2 = pairs(own2, near0, across0)
    across2 = middle(own2, near0, across0)
    out0 = pairs(jnp.where(at_end, chunk(0), across0), near1, across1)
    across3 = middle(own3, near1, across1)
    out1 = pairs(jnp.where(at_end, chunk(1), across1), near2, across2)
    far0 = middle(near0, near2, across2)
    first = products(
        [[[full(own0)], [full(near0)]], [[full(own1)], [full(near1)]], [[full(own2), upper(own3, None)], [full(near2)]]],
        right,
        extent,
        side,
    )
    out2 = pairs(jnp.where(at_end, own3, across2), out0, across3)
    far1 = middle(near1, out0, across3)
    far2 = middle(near2, out1, far0, first)
    far_out0 = pairs(jnp.where(at_end, chunk(2), far0), out1, far0, first)
    far3 = middle(out2, far1)
    far_out1 = pairs(jnp.where(at_end, chunk(3), far1), out2, far1)
    second = products(
        [
            [[full(across0), at_ends(out0)]],
            [[full(across1), at_ends(out1)]],
            [
                [full(across2), at_ends(out2), upper(across3, None)],
                [upper(far3, None)],
                [upper(out2, INNER)],
            ],
        ],
        right,
        extent,
        side,
    )
    for_end = lambda panel, i: products(
        [[], [], [[(0, piece, None, i)] for piece in (own3, across3, far3)]],
        panel.reshape(1, depth, width),
        depth,
        side,
        resident=True,
    )[:, 2]
    to_ends = for_end(out0, 0) + for_end(out1, 1)
    third = products([[[full(far0), at_ends(far_out0)]], [], []], right, extent, side)
    to_ends = to_ends + for_end(far_out0, 2)
    far_out2 = pairs(far2, far_out0, far2, second, third, to_ends)
    from_neighbour = outward(to_ends + for_end(far_out1, 3))
    fourth, panel = products([[], [[full(far1), at_ends(far_out1)]], []], right, extent, side, keep=half)
    fifth = products([[], [], [[full(far2), at_ends(far_out2)]]], panel, half, side, resident=True)

    shards = jnp.stack([first[0], first[1], second[0], third[0] + fourth[0] + fifth[0]])
    shards = shards.at[1, 2].add(second[2, 2]).at[3, 2].add(second[1, 2])
    shards = shards.at[1:, 2].add(from_neighbour)
    slots = lambda *at: functools.reduce(lambda rest, i: jnp.where(place == i, at[i], rest), range(3), at[3])
    where_is = (slots(0, 1, 3, 3), slots(1, 0, 2, 2), slots(2, 2, 0, 1), slots(3, 3, 1, 0))
    return jnp.stack([lax.dynamic_index_in_dim(shards, slot, 0, False) for slot in where_is])


def on_device(cols, rows, left_panels, right_panels, window_tiles):
    height, width = window_tiles.shape[1:]
    if cols == 4:
        shards = line_of_four(left_panels, right_panels)
    else:
        gathered = lax.all_gather(left_panels, "col", axis=1, tiled=True)
        lefts = [[[(0, blocked(gathered[a]), None, None)]] for a in range(ORDERS)]
        shards = products(lefts, right_panels, right_panels.shape[1], jnp.zeros((1,), jnp.int32))
    blocks = shards.reshape(-1, ORDERS, shards.shape[2] // height, height, width)
    blocks = jnp.swapaxes(blocks, 1, 2).reshape(rows, ORDERS, height, width)
    return 2.0 * window_tiles - sum_over_row(blocks, rows)


def solution(mesh):
    return jax.shard_map(
        functools.partial(on_device, mesh.shape["col"], mesh.shape["row"]),
        mesh=mesh,
        in_specs=(P(None, "col", "row"), P(None, "row", "col"), P(None, "row", "col")),
        out_specs=P(None, "row", "col"),
        check_vma=False,
    )
```

```python
import functools

import jax
import jax.numpy as jnp
from jax import lax
from jax.experimental import pallas as pl
from jax.experimental.pallas import tpu as pltpu
from jax.sharding import PartitionSpec as P

ORDERS = 3
LANES, SUBLANES = 128, 8
TILE = 1024
VMEM_LIMIT = 48 * 1024 * 1024


def halves(values):
    high = values.astype(jnp.bfloat16)
    return high, (values - high.astype(jnp.float32)).astype(jnp.bfloat16)


def blocked(left):
    height, extent = left.shape
    return left.reshape(height // SUBLANES, SUBLANES, extent // LANES, LANES).transpose(0, 2, 1, 3)


def unblocked(blocks):
    return jnp.concatenate(
        [jnp.concatenate([blocks[a, c] for c in range(blocks.shape[1])], axis=1) for a in range(blocks.shape[0])], axis=0
    )


def products_kernel(layout, steps, orders, keep, only, side_ref, *refs):
    count = sum(len(terms) for sources in layout for terms in sources)
    left_refs, right_ref, out_ref = refs[:count], refs[count], refs[count + 1]
    kept_ref = refs[count + 2] if keep else None
    scratch = refs[count + 2 + bool(keep) :]
    totals, held = scratch[:orders], scratch[orders:]
    sources_of = [len(sources) for sources in layout]
    tile = right_ref.shape[1] // steps if not held else held[0].shape[1] // steps
    columns = tile // LANES

    def arrival(step):
        rows = pl.ds(step * tile, tile)
        return pltpu.make_async_copy(right_ref.at[:orders, rows], held[0].at[:, rows], held[1].at[step])

    def add_up():
        if held:
            for step in range(steps):
                arrival(step).start()
        panels = held[0] if held else right_ref

        @pl.loop(0, steps)
        def _(step):
            if held:
                arrival(step).wait()
            if keep:

                @pl.when(step < keep // tile)
                def _():
                    rows = pl.ds(step * tile, tile)
                    kept_ref[0, rows] = panels[0, rows]
            rows, place = [], 0
            for sources in layout:
                for terms in sources:
                    piece = None
                    for first, tiles, skip, side in terms:
                        at = skip + (jnp.clip(step - first, 0, tiles - 1) if tiles < steps else step)
                        term = unblocked(left_refs[place][:, pl.ds(at * columns, columns)])
                        counts = None
                        if tiles < steps:
                            counts = (step >= first) & (step < first + tiles)
                        if side is not None:
                            here = side_ref[0] == side
                            counts = here if counts is None else counts & here
                        if counts is not None:
                            term = jnp.where(counts, term, 0.0)
                        piece = term if piece is None else piece + term
                        place += 1
                    rows.extend(halves(piece))
            stacked = jnp.concatenate(rows, axis=0)
            height = rows[0].shape[0]
            for order, parts in enumerate(totals):
                panel = jnp.concatenate(halves(panels[order, pl.ds(step * tile, tile), :]), axis=1)
                used = 2 * height * sum(sources_of[: ORDERS - order])
                parts[step] = jnp.dot(stacked[:used], panel, preferred_element_type=jnp.float32)

        height, width = out_ref.shape[2:]
        sums = [jnp.sum(parts[...], axis=0) for parts in totals]
        for source in range(max(sources_of)):
            for out_order in range(ORDERS):
                value = jnp.zeros((height, width), jnp.float32)
                first_row = 0
                for left_order in range(ORDERS):
                    right_order = out_order - left_order
                    if 0 <= right_order < len(totals) and source < sources_of[left_order]:
                        top = (first_row + source) * 2 * height
                        block = sums[right_order][top : top + 2 * height]
                        block = block[:height] + block[height:]
                        value = value + (block[:, :width] + block[:, width:])
                    first_row += sources_of[left_order]
                out_ref[source, out_order] = value

    if only is None:
        add_up()
    else:
        here = side_ref[0] == only
        pl.when(here)(add_up)

        @pl.when(jnp.logical_not(here))
        def _():
            out_ref[...] = jnp.zeros_like(out_ref)


def products(lefts, right, extent, side, resident=False, keep=0, only=None):
    flat = [term for sources in lefts for terms in sources for term in terms]
    height = flat[0][1].shape[0] * SUBLANES
    width = right.shape[2]
    tile = min(TILE, extent)
    steps = extent // tile
    tiles_of = lambda array, part: (extent if part is not None else array.shape[1] * LANES) // tile
    layout = [
        [
            [(first // tile, tiles_of(array, part), (part or 0) * steps, on) for first, array, on, part in terms]
            for terms in sources
        ]
        for sources in lefts
    ]
    sources_of = [len(sources) for sources in lefts]
    orders = min(ORDERS - min(a for a in range(ORDERS) if sources_of[a]), right.shape[0])
    rows_of = [2 * height * sum(sources_of[: ORDERS - order]) for order in range(orders)]
    in_vmem = pl.BlockSpec(memory_space=pltpu.VMEM)
    held = [] if resident else [
        pltpu.VMEM((orders, extent, width), jnp.float32),
        pltpu.SemaphoreType.DMA((steps,)),
    ]
    out = jax.ShapeDtypeStruct((max(sources_of), ORDERS, height, width), jnp.float32)
    kept = jax.ShapeDtypeStruct((1, keep, width), jnp.float32)
    return pl.pallas_call(
        functools.partial(products_kernel, layout, steps, orders, keep, only),
        in_specs=[pl.BlockSpec(memory_space=pltpu.SMEM)]
        + [in_vmem] * len(flat)
        + [in_vmem if resident else pl.BlockSpec(memory_space=pltpu.HBM)],
        out_specs=(in_vmem, in_vmem) if keep else in_vmem,
        out_shape=(out, kept) if keep else out,
        scratch_shapes=[pltpu.VMEM((steps, rows, 2 * width), jnp.float32) for rows in rows_of] + held,
        compiler_params=pltpu.CompilerParams(vmem_limit_bytes=VMEM_LIMIT),
        cost_estimate=pl.CostEstimate(
            flops=int(3 * 4 * sum(rows_of) * extent * width),
            bytes_accessed=int(3 * 4 * (sum(term[1].size for term in flat) + orders * extent * width)),
            transcendentals=0,
        ),
    )(side, *[term[1] for term in flat], right)


def sum_over_row(blocks, row_size):
    if row_size != 8:
        return lax.psum_scatter(blocks, "row", scatter_dimension=0, tiled=True)[0]
    me = lax.axis_index("row")
    pairs = blocks.reshape((4, 2) + blocks.shape[1:])
    core, chip = me % 2, me // 2
    keep = lax.dynamic_index_in_dim(pairs, core, 1, False)
    give = lax.dynamic_index_in_dim(pairs, 1 - core, 1, False)
    mine = keep + lax.ppermute(give, "row", [(i, i ^ 1) for i in range(8)])
    total = lax.dynamic_index_in_dim(mine, chip, 0, False)
    for offset in (3, 1, 2):
        block = lax.dynamic_index_in_dim(mine, chip ^ offset, 0, False)
        total = total + lax.ppermute(block, "row", [(i, i ^ (2 * offset)) for i in range(8)])
    return total


def after(array, *earlier):
    return lax.optimization_barrier((array, *earlier))[0]


END, INNER = 1, 0


def line_of_four(left, right):
    place = lax.axis_index("col")
    at_end = (place == 0) | (place == 3)
    side = at_end.astype(jnp.int32).reshape(1)
    pairs = lambda array, *earlier: lax.ppermute(after(array, *earlier), "col", [(0, 1), (1, 0), (2, 3), (3, 2)])
    middle = lambda array, *earlier: lax.ppermute(after(array, *earlier), "col", [(1, 2), (2, 1)])
    outward = lambda array: lax.ppermute(array, "col", [(1, 0), (2, 3)])
    extent = left.shape[2]
    half = extent // 2
    own0, own1 = blocked(left[0]), blocked(left[1])
    left2 = after(left, own0, own1)[2]
    own2, own3 = blocked(left2[:, :half]), blocked(left2[:, half:])
    width = right.shape[2]
    depth = own0.size // width
    chunk = lambda i: right[0, half + i * depth : half + (i + 1) * depth].reshape(own0.shape)
    full = lambda array: (0, array, None, None)
    at_ends = lambda array: (0, array, END, None)
    upper = lambda array, on: (half, array, on, None)
    for_end = lambda panel, i, side: products(
        [[], [], [[(0, piece, None, i)] for piece in (own3, across3, far3)]],
        panel.reshape(1, depth, width),
        depth,
        side,
        resident=True,
        only=INNER,
    )[:, 2]

    near0 = pairs(own0)
    across0 = middle(own0)
    near1 = pairs(own1)
    across1 = middle(own1)
    near2 = pairs(own2, near0, across0)
    across3 = middle(own3, near1, across1)
    across2 = middle(own2, near0, across0)
    far0 = middle(near0, near2, across2)
    out0 = pairs(jnp.where(at_end, chunk(0), across0), near1, across1)
    out1 = pairs(jnp.where(at_end, chunk(1), across1), near2)
    first = products([[[full(own0)], [full(near0)]], [[full(own1)], [full(near1)]], [[full(own2), upper(own3, None)], [full(near2)]]], right, extent, side)
    out2 = pairs(jnp.where(at_end, own3, across2), out0, across3, first)
    far2 = middle(near2, out1, far0)
    far1 = middle(near1, out0, across3, first)
    far_out0 = pairs(jnp.where(at_end, chunk(2), far0))
    second = products([[[full(across0), at_ends(out0)]], [[full(across1), at_ends(out1)]], []], right, extent, side)
    far3 = middle(out2, far1, second)
    third = products([[[full(far0), at_ends(far_out0)]], [[full(far1)]], [[full(far2), upper(far3, None)], [full(across2), at_ends(out2), upper(across3, None)], [upper(out2, INNER)]]], right, extent, side)
    far_out1 = pairs(jnp.where(at_end, chunk(3), far1), out2, far1, second)
    end0 = for_end(out0, 0, side)
    end1 = for_end(out1, 1, side)
    end2 = for_end(far_out0, 2, side)
    far_out2 = pairs(far2, far_out0, far2)
    end3 = for_end(far_out1, 3, side)
    back = outward(after(end0 + end1 + end2 + end3, third))
    fourth, panel = products([[], [[full(far_out1)]], []], right, extent, side, keep=half, only=END)
    fifth = products([[], [], [[full(far_out2)]]], panel, half, side, resident=True, only=END)

    shards = jnp.stack([first[0], first[1], second[0], third[0] + fourth[0] + fifth[0]])
    shards = shards.at[1, 2].add(third[2, 2]).at[2, 2].add(third[1, 2])
    shards = shards.at[1:, 2].add(back)
    slots = lambda *at: functools.reduce(lambda rest, i: jnp.where(place == i, at[i], rest), range(3), at[3])
    where_is = (slots(0, 1, 3, 3), slots(1, 0, 2, 2), slots(2, 2, 0, 1), slots(3, 3, 1, 0))
    return jnp.stack([lax.dynamic_index_in_dim(shards, slot, 0, False) for slot in where_is])


def on_device(cols, rows, left_panels, right_panels, window_tiles):
    height, width = window_tiles.shape[1:]
    chunks = right_panels.shape[1] // 2 * width // left_panels[0].size
    if (cols, chunks) == (4, 4):
        shards = line_of_four(left_panels, right_panels)
    else:
        gathered = lax.all_gather(left_panels, "col", axis=1, tiled=True)
        lefts = [[[(0, blocked(gathered[a]), None, None)]] for a in range(ORDERS)]
        shards = products(lefts, right_panels, right_panels.shape[1], jnp.zeros((1,), jnp.int32))
    blocks = shards.reshape(-1, ORDERS, shards.shape[2] // height, height, width)
    blocks = jnp.swapaxes(blocks, 1, 2).reshape(rows, ORDERS, height, width)
    return 2.0 * window_tiles - sum_over_row(blocks, rows)


def solution(mesh):
    return jax.shard_map(
        functools.partial(on_device, mesh.shape["col"], mesh.shape["row"]),
        mesh=mesh,
        in_specs=(P(None, "col", "row"), P(None, "row", "col"), P(None, "row", "col")),
        out_specs=P(None, "row", "col"),
        check_vma=False,
    )
```

```python
import functools

import jax
import jax.numpy as jnp
from jax import lax
from jax.experimental import pallas as pl
from jax.experimental.pallas import tpu as pltpu
from jax.sharding import PartitionSpec as P

ORDERS = 3
LANES, SUBLANES = 128, 8
TILE = 1024
VMEM_LIMIT = 48 * 1024 * 1024


def halves(values):
    high = values.astype(jnp.bfloat16)
    return high, (values - high.astype(jnp.float32)).astype(jnp.bfloat16)


def blocked(left):
    height, extent = left.shape
    return left.reshape(height // SUBLANES, SUBLANES, extent // LANES, LANES).transpose(0, 2, 1, 3)


def unblocked(blocks):
    return jnp.concatenate(
        [jnp.concatenate([blocks[a, c] for c in range(blocks.shape[1])], axis=1) for a in range(blocks.shape[0])], axis=0
    )


def products_kernel(layout, steps, orders, keep, only, side_ref, *refs):
    count = sum(len(terms) for sources in layout for terms in sources)
    left_refs, right_ref, out_ref = refs[:count], refs[count], refs[count + 1]
    kept_ref = refs[count + 2] if keep else None
    scratch = refs[count + 2 + bool(keep) :]
    totals, held = scratch[:orders], scratch[orders:]
    sources_of = [len(sources) for sources in layout]
    tile = right_ref.shape[1] // steps if not held else held[0].shape[1] // steps
    columns = tile // LANES

    def arrival(step):
        rows = pl.ds(step * tile, tile)
        return pltpu.make_async_copy(right_ref.at[:orders, rows], held[0].at[:, rows], held[1].at[step])

    def add_up():
        if held:
            for step in range(steps):
                arrival(step).start()
        panels = held[0] if held else right_ref

        @pl.loop(0, steps)
        def _(step):
            if held:
                arrival(step).wait()
            if keep:

                @pl.when(step < keep // tile)
                def _():
                    rows = pl.ds(step * tile, tile)
                    kept_ref[0, rows] = panels[0, rows]
            rows, place = [], 0
            for sources in layout:
                for terms in sources:
                    piece = None
                    for first, tiles, skip, side in terms:
                        at = skip + (jnp.clip(step - first, 0, tiles - 1) if tiles < steps else step)
                        term = unblocked(left_refs[place][:, pl.ds(at * columns, columns)])
                        counts = None
                        if tiles < steps:
                            counts = (step >= first) & (step < first + tiles)
                        if side is not None:
                            here = side_ref[0] == side
                            counts = here if counts is None else counts & here
                        if counts is not None:
                            term = jnp.where(counts, term, 0.0)
                        piece = term if piece is None else piece + term
                        place += 1
                    rows.extend(halves(piece))
            stacked = jnp.concatenate(rows, axis=0)
            height = rows[0].shape[0]
            for order, parts in enumerate(totals):
                panel = jnp.concatenate(halves(panels[order, pl.ds(step * tile, tile), :]), axis=1)
                used = 2 * height * sum(sources_of[: ORDERS - order])
                parts[step] = jnp.dot(stacked[:used], panel, preferred_element_type=jnp.float32)

        height, width = out_ref.shape[2:]
        sums = [jnp.sum(parts[...], axis=0) for parts in totals]
        for source in range(max(sources_of)):
            for out_order in range(ORDERS):
                value = jnp.zeros((height, width), jnp.float32)
                first_row = 0
                for left_order in range(ORDERS):
                    right_order = out_order - left_order
                    if 0 <= right_order < len(totals) and source < sources_of[left_order]:
                        top = (first_row + source) * 2 * height
                        block = sums[right_order][top : top + 2 * height]
                        block = block[:height] + block[height:]
                        value = value + (block[:, :width] + block[:, width:])
                    first_row += sources_of[left_order]
                out_ref[source, out_order] = value

    if only is None:
        add_up()
    else:
        here = side_ref[0] == only
        pl.when(here)(add_up)

        @pl.when(jnp.logical_not(here))
        def _():
            out_ref[...] = jnp.zeros_like(out_ref)


def products(lefts, right, extent, side, resident=False, keep=0, only=None):
    flat = [term for sources in lefts for terms in sources for term in terms]
    height = flat[0][1].shape[0] * SUBLANES
    width = right.shape[2]
    tile = min(TILE, extent)
    steps = extent // tile
    tiles_of = lambda array, part: (extent if part is not None else array.shape[1] * LANES) // tile
    layout = [
        [
            [(first // tile, tiles_of(array, part), (part or 0) * steps, on) for first, array, on, part in terms]
            for terms in sources
        ]
        for sources in lefts
    ]
    sources_of = [len(sources) for sources in lefts]
    orders = min(ORDERS - min(a for a in range(ORDERS) if sources_of[a]), right.shape[0])
    rows_of = [2 * height * sum(sources_of[: ORDERS - order]) for order in range(orders)]
    in_vmem = pl.BlockSpec(memory_space=pltpu.VMEM)
    held = [] if resident else [
        pltpu.VMEM((orders, extent, width), jnp.float32),
        pltpu.SemaphoreType.DMA((steps,)),
    ]
    out = jax.ShapeDtypeStruct((max(sources_of), ORDERS, height, width), jnp.float32)
    kept = jax.ShapeDtypeStruct((1, keep, width), jnp.float32)
    return pl.pallas_call(
        functools.partial(products_kernel, layout, steps, orders, keep, only),
        in_specs=[pl.BlockSpec(memory_space=pltpu.SMEM)]
        + [in_vmem] * len(flat)
        + [in_vmem if resident else pl.BlockSpec(memory_space=pltpu.HBM)],
        out_specs=(in_vmem, in_vmem) if keep else in_vmem,
        out_shape=(out, kept) if keep else out,
        scratch_shapes=[pltpu.VMEM((steps, rows, 2 * width), jnp.float32) for rows in rows_of] + held,
        compiler_params=pltpu.CompilerParams(vmem_limit_bytes=VMEM_LIMIT),
        cost_estimate=pl.CostEstimate(
            flops=int(3 * 4 * sum(rows_of) * extent * width),
            bytes_accessed=int(3 * 4 * (sum(term[1].size for term in flat) + orders * extent * width)),
            transcendentals=0,
        ),
    )(side, *[term[1] for term in flat], right)


def after(array, *earlier):
    return lax.optimization_barrier((array, *earlier))[0]


def sum_over_row(blocks, row_size):
    if row_size != 8:
        return lax.psum_scatter(blocks, "row", scatter_dimension=0, tiled=True)[0]
    me = lax.axis_index("row")
    pairs = blocks.reshape((4, 2) + blocks.shape[1:])
    core, chip = me % 2, me // 2
    to = lambda array, offset: lax.ppermute(array, "row", [(i, i ^ offset) for i in range(8)])
    pick = lambda array, index, axis=0: lax.dynamic_index_in_dim(array, index, axis, False)
    mine = pick(pairs, core, 1) + to(pick(pairs, 1 - core, 1), 1)
    early = to(pick(pairs, chip ^ 1), 2)
    one = to(pick(mine, chip ^ 2), 4)
    two = to(pick(mine, chip ^ 3), 6)
    early = after(early, two)
    return pick(mine, chip) + one + two + pick(early, core) + to(pick(early, 1 - core), 1)


END, INNER = 1, 0


def line_of_four(left, right):
    place = lax.axis_index("col")
    at_end = (place == 0) | (place == 3)
    side = at_end.astype(jnp.int32).reshape(1)
    pairs = lambda array, *earlier: lax.ppermute(after(array, *earlier), "col", [(0, 1), (1, 0), (2, 3), (3, 2)])
    middle = lambda array, *earlier: lax.ppermute(after(array, *earlier), "col", [(1, 2), (2, 1)])
    outward = lambda array: lax.ppermute(array, "col", [(1, 0), (2, 3)])
    extent = left.shape[2]
    half = extent // 2
    own0 = blocked(left[0])
    left1 = after(left, own0)
    own1, own2, own3 = blocked(left1[1]), blocked(left1[2, :, :half]), blocked(left1[2, :, half:])
    width = right.shape[2]
    depth = own0.size // width
    chunk = lambda i: right[0, half + i * depth : half + (i + 1) * depth].reshape(own0.shape)
    full = lambda array: (0, array, None, None)
    at_ends = lambda array: (0, array, END, None)
    upper = lambda array, on: (half, array, on, None)
    for_end = lambda panel, i, side: products(
        [[], [], [[(0, piece, None, i)] for piece in (own3, across3, far3)]],
        panel.reshape(1, depth, width),
        depth,
        side,
        resident=True,
        only=INNER,
    )[:, 2]

    near0 = pairs(own0)
    across0 = middle(own0)
    near1 = pairs(own1)
    across1 = middle(own1)
    near2 = pairs(own2, near0, across0)
    across3 = middle(own3, near1, across1)
    across2 = middle(own2, near0, across0)
    far0 = middle(near0, near2, across2)
    out0 = pairs(jnp.where(at_end, chunk(0), across0), near1, across1)
    out1 = pairs(jnp.where(at_end, chunk(1), across1), near2)
    first = products([[[full(own0)], [full(near0)]], [[full(own1)], [full(near1)]], [[full(own2), upper(own3, None)], [full(near2)]]], right, extent, side)
    out2 = pairs(jnp.where(at_end, own3, across2), out0, across3, first)
    far2 = middle(near2, out1, far0)
    far1 = middle(near1, out0, across3, first)
    far_out0 = pairs(jnp.where(at_end, chunk(2), far0))
    second = products([[[full(across0), at_ends(out0)]], [[full(across1), at_ends(out1)]], []], right, extent, side)
    far3 = middle(out2, far1, second)
    third = products([[[full(far0), at_ends(far_out0)]], [[full(far1)]], [[full(far2), upper(far3, None)], [full(across2), at_ends(out2), upper(across3, None)], [upper(out2, INNER)]]], right, extent, side)
    far_out1 = pairs(jnp.where(at_end, chunk(3), far1), out2, far1, second)
    end0 = for_end(out0, 0, side)
    end1 = for_end(out1, 1, side)
    end2 = for_end(far_out0, 2, side)
    far_out2 = pairs(far2, far_out0, far2)
    end3 = for_end(far_out1, 3, side)
    back = outward(after(end0 + end1 + end2 + end3, third))
    fourth, panel = products([[], [[full(far_out1)]], []], right, extent, side, keep=half, only=END)
    fifth = products([[], [], [[full(far_out2)]]], panel, half, side, resident=True, only=END)

    shards = jnp.stack([first[0], first[1], second[0], third[0] + fourth[0] + fifth[0]])
    shards = shards.at[1, 2].add(third[2, 2]).at[2, 2].add(third[1, 2])
    shards = shards.at[1:, 2].add(back)
    slots = lambda *at: functools.reduce(lambda rest, i: jnp.where(place == i, at[i], rest), range(3), at[3])
    where_is = (slots(0, 1, 3, 3), slots(1, 0, 2, 2), slots(2, 2, 0, 1), slots(3, 3, 1, 0))
    return jnp.stack([lax.dynamic_index_in_dim(shards, slot, 0, False) for slot in where_is])


def on_device(cols, rows, left_panels, right_panels, window_tiles):
    height, width = window_tiles.shape[1:]
    chunks = right_panels.shape[1] // 2 * width // left_panels[0].size
    if (cols, chunks) == (4, 4):
        shards = line_of_four(left_panels, right_panels)
    else:
        gathered = lax.all_gather(left_panels, "col", axis=1, tiled=True)
        lefts = [[[(0, blocked(gathered[a]), None, None)]] for a in range(ORDERS)]
        shards = products(lefts, right_panels, right_panels.shape[1], jnp.zeros((1,), jnp.int32))
    blocks = shards.reshape(-1, ORDERS, shards.shape[2] // height, height, width)
    blocks = jnp.swapaxes(blocks, 1, 2).reshape(rows, ORDERS, height, width)
    return 2.0 * window_tiles - sum_over_row(blocks, rows)


def solution(mesh):
    return jax.shard_map(
        functools.partial(on_device, mesh.shape["col"], mesh.shape["row"]),
        mesh=mesh,
        in_specs=(P(None, "col", "row"), P(None, "row", "col"), P(None, "row", "col")),
        out_specs=P(None, "row", "col"),
        check_vma=False,
    )
```

```python
import functools

import jax
import jax.numpy as jnp
from jax import lax
from jax.experimental import pallas as pl
from jax.experimental.pallas import tpu as pltpu
from jax.sharding import PartitionSpec as P

ORDERS = 3
LANES, SUBLANES = 128, 8
TILE = 1024
VMEM_LIMIT = 48 * 1024 * 1024
COST_WEIGHT = 3


def halves(values):
    high = values.astype(jnp.bfloat16)
    return high, (values - high.astype(jnp.float32)).astype(jnp.bfloat16)


def blocked(left):
    height, extent = left.shape
    return left.reshape(height // SUBLANES, SUBLANES, extent // LANES, LANES).transpose(0, 2, 1, 3)


def unblocked(blocks):
    return jnp.concatenate(
        [jnp.concatenate([blocks[a, c] for c in range(blocks.shape[1])], axis=1) for a in range(blocks.shape[0])], axis=0
    )


def products_kernel(layout, steps, orders, keep, only, side_ref, *refs):
    count = sum(len(terms) for sources in layout for terms in sources)
    left_refs, right_ref, out_ref = refs[:count], refs[count], refs[count + 1]
    kept_ref = refs[count + 2] if keep else None
    scratch = refs[count + 2 + bool(keep) :]
    totals, held = scratch[:orders], scratch[orders:]
    sources_of = [len(sources) for sources in layout]
    tile = right_ref.shape[1] // steps if not held else held[0].shape[1] // steps
    columns = tile // LANES

    def arrival(step):
        rows = pl.ds(step * tile, tile)
        return pltpu.make_async_copy(right_ref.at[:orders, rows], held[0].at[:, rows], held[1].at[step])

    def add_up():
        if held:
            for step in range(steps):
                arrival(step).start()
        panels = held[0] if held else right_ref

        @pl.loop(0, steps)
        def _(step):
            if held:
                arrival(step).wait()
            if keep:

                @pl.when(step < keep // tile)
                def _():
                    rows = pl.ds(step * tile, tile)
                    kept_ref[0, rows] = panels[0, rows]
            rows, place = [], 0
            for sources in layout:
                for terms in sources:
                    piece = None
                    for first, tiles, skip, side in terms:
                        at = skip + (jnp.clip(step - first, 0, tiles - 1) if tiles < steps else step)
                        term = unblocked(left_refs[place][:, pl.ds(at * columns, columns)])
                        counts = None
                        if tiles < steps:
                            counts = (step >= first) & (step < first + tiles)
                        if side is not None:
                            here = side_ref[0] == side
                            counts = here if counts is None else counts & here
                        if counts is not None:
                            term = jnp.where(counts, term, 0.0)
                        piece = term if piece is None else piece + term
                        place += 1
                    rows.extend(halves(piece))
            stacked = jnp.concatenate(rows, axis=0)
            height = rows[0].shape[0]
            for order, parts in enumerate(totals):
                panel = jnp.concatenate(halves(panels[order, pl.ds(step * tile, tile), :]), axis=1)
                used = 2 * height * sum(sources_of[: ORDERS - order])
                parts[step] = jnp.dot(stacked[:used], panel, preferred_element_type=jnp.float32)

        height, width = out_ref.shape[2:]
        sums = [jnp.sum(parts[...], axis=0) for parts in totals]
        for source in range(max(sources_of)):
            for out_order in range(ORDERS):
                value = jnp.zeros((height, width), jnp.float32)
                first_row = 0
                for left_order in range(ORDERS):
                    right_order = out_order - left_order
                    if 0 <= right_order < len(totals) and source < sources_of[left_order]:
                        top = (first_row + source) * 2 * height
                        block = sums[right_order][top : top + 2 * height]
                        block = block[:height] + block[height:]
                        value = value + (block[:, :width] + block[:, width:])
                    first_row += sources_of[left_order]
                out_ref[source, out_order] = value

    if only is None:
        add_up()
    else:
        here = side_ref[0] == only
        pl.when(here)(add_up)

        @pl.when(jnp.logical_not(here))
        def _():
            out_ref[...] = jnp.zeros_like(out_ref)


def products(lefts, right, extent, side, resident=False, keep=0, only=None):
    flat = [term for sources in lefts for terms in sources for term in terms]
    height = flat[0][1].shape[0] * SUBLANES
    width = right.shape[2]
    tile = min(TILE, extent)
    steps = extent // tile
    tiles_of = lambda array, part: (extent if part is not None else array.shape[1] * LANES) // tile
    layout = [
        [
            [(first // tile, tiles_of(array, part), (part or 0) * steps, on) for first, array, on, part in terms]
            for terms in sources
        ]
        for sources in lefts
    ]
    sources_of = [len(sources) for sources in lefts]
    orders = min(ORDERS - min(a for a in range(ORDERS) if sources_of[a]), right.shape[0])
    rows_of = [2 * height * sum(sources_of[: ORDERS - order]) for order in range(orders)]
    in_vmem = pl.BlockSpec(memory_space=pltpu.VMEM)
    held = [] if resident else [
        pltpu.VMEM((orders, extent, width), jnp.float32),
        pltpu.SemaphoreType.DMA((steps,)),
    ]
    out = jax.ShapeDtypeStruct((max(sources_of), ORDERS, height, width), jnp.float32)
    kept = jax.ShapeDtypeStruct((1, keep, width), jnp.float32)
    return pl.pallas_call(
        functools.partial(products_kernel, layout, steps, orders, keep, only),
        in_specs=[pl.BlockSpec(memory_space=pltpu.SMEM)]
        + [in_vmem] * len(flat)
        + [in_vmem if resident else pl.BlockSpec(memory_space=pltpu.HBM)],
        out_specs=(in_vmem, in_vmem) if keep else in_vmem,
        out_shape=(out, kept) if keep else out,
        scratch_shapes=[pltpu.VMEM((steps, rows, 2 * width), jnp.float32) for rows in rows_of] + held,
        compiler_params=pltpu.CompilerParams(vmem_limit_bytes=VMEM_LIMIT),
        cost_estimate=pl.CostEstimate(
            flops=COST_WEIGHT * 4 * sum(rows_of) * extent * width,
            bytes_accessed=COST_WEIGHT * 4 * (sum(term[1].size for term in flat) + orders * extent * width),
            transcendentals=0,
        ),
    )(side, *[term[1] for term in flat], right)


def after(array, *earlier):
    return lax.optimization_barrier((array, *earlier))[0]


def sum_over_row(blocks, row_size):
    if row_size != 8:
        return lax.psum_scatter(blocks, "row", scatter_dimension=0, tiled=True)[0]
    me = lax.axis_index("row")
    pairs = blocks.reshape((4, 2) + blocks.shape[1:])
    core, chip = me % 2, me // 2
    to = lambda array, offset: lax.ppermute(array, "row", [(i, i ^ offset) for i in range(8)])
    pick = lambda array, index, axis=0: lax.dynamic_index_in_dim(array, index, axis, False)
    mine = pick(pairs, core, 1) + to(pick(pairs, 1 - core, 1), 1)
    early = to(pick(pairs, chip ^ 1), 2)
    one = to(pick(mine, chip ^ 2), 4)
    two = to(pick(mine, chip ^ 3), 6)
    early = after(early, two)
    return pick(mine, chip) + one + two + pick(early, core) + to(pick(early, 1 - core), 1)


END, INNER = 1, 0


def line_of_four(left, right):
    place = lax.axis_index("col")
    at_end = (place == 0) | (place == 3)
    side = at_end.astype(jnp.int32).reshape(1)
    pairs = lambda array, *earlier: lax.ppermute(after(array, *earlier), "col", [(0, 1), (1, 0), (2, 3), (3, 2)])
    middle = lambda array, *earlier: lax.ppermute(after(array, *earlier), "col", [(1, 2), (2, 1)])
    outward = lambda array: lax.ppermute(array, "col", [(1, 0), (2, 3)])
    extent = left.shape[2]
    half = extent // 2
    own0 = blocked(left[0])
    left1 = after(left, own0)
    own1, own2, own3 = blocked(left1[1]), blocked(left1[2, :, :half]), blocked(left1[2, :, half:])
    width = right.shape[2]
    depth = own0.size // width
    chunk = lambda i: right[0, half + i * depth : half + (i + 1) * depth].reshape(own0.shape)
    full = lambda array: (0, array, None, None)
    at_ends = lambda array: (0, array, END, None)
    upper = lambda array, on: (half, array, on, None)
    for_end = lambda panel, i, side: products(
        [[], [], [[(0, piece, None, i)] for piece in (own3, across3, far3)]],
        panel.reshape(1, depth, width),
        depth,
        side,
        resident=True,
        only=INNER,
    )[:, 2]

    near0 = pairs(own0)
    across0 = middle(own0)
    near1 = pairs(own1)
    across1 = middle(own1)
    near2 = pairs(own2, near0, across0)
    across3 = middle(own3, near1, across1)
    across2 = middle(own2, near0, across0)
    far0 = middle(near0, near2, across2)
    out0 = pairs(jnp.where(at_end, chunk(0), across0), near1, across1)
    out1 = pairs(jnp.where(at_end, chunk(1), across1), near2)
    first = products(
        [
            [[full(own0)], [full(near0)]],
            [[full(own1)], [full(near1)]],
            [[full(own2), upper(own3, None)], [full(near2)]],
        ],
        right,
        extent,
        side,
    )
    out2 = pairs(jnp.where(at_end, own3, across2), out0, across3, first)
    far2 = middle(near2, out1, far0)
    far1 = middle(near1, out0, across3, first)
    far_out0 = pairs(jnp.where(at_end, chunk(2), far0))
    second = products(
        [[[full(across0), at_ends(out0)]], [[full(across1), at_ends(out1)]], []], right, extent, side
    )
    far3 = middle(out2, far1, second)
    third = products(
        [
            [[full(far0), at_ends(far_out0)]],
            [[full(far1)]],
            [
                [full(far2), upper(far3, None)],
                [full(across2), at_ends(out2), upper(across3, None)],
                [upper(out2, INNER)],
            ],
        ],
        right,
        extent,
        side,
    )
    far_out1 = pairs(jnp.where(at_end, chunk(3), far1), out2, far1, second)
    end0 = for_end(out0, 0, side)
    end1 = for_end(out1, 1, side)
    end2 = for_end(far_out0, 2, side)
    far_out2 = pairs(far2, far_out0, far2)
    end3 = for_end(far_out1, 3, side)
    back = outward(after(end0 + end1 + end2 + end3, third))
    fourth, panel = products([[], [[full(far_out1)]], []], right, extent, side, keep=half, only=END)
    fifth = products([[], [], [[full(far_out2)]]], panel, half, side, resident=True, only=END)

    shards = jnp.stack([first[0], first[1], second[0], third[0] + fourth[0] + fifth[0]])
    shards = shards.at[1, 2].add(third[2, 2]).at[2, 2].add(third[1, 2])
    shards = shards.at[1:, 2].add(back)
    slots = lambda *at: functools.reduce(lambda rest, i: jnp.where(place == i, at[i], rest), range(3), at[3])
    where_is = (slots(0, 1, 3, 3), slots(1, 0, 2, 2), slots(2, 2, 0, 1), slots(3, 3, 1, 0))
    return jnp.stack([lax.dynamic_index_in_dim(shards, slot, 0, False) for slot in where_is])


def on_device(cols, rows, left_panels, right_panels, window_tiles):
    height, width = window_tiles.shape[1:]
    chunks = right_panels.shape[1] // 2 * width // left_panels[0].size
    if (cols, chunks) == (4, 4):
        shards = line_of_four(left_panels, right_panels)
    else:
        gathered = lax.all_gather(left_panels, "col", axis=1, tiled=True)
        lefts = [[[(0, blocked(gathered[a]), None, None)]] for a in range(ORDERS)]
        shards = products(lefts, right_panels, right_panels.shape[1], jnp.zeros((1,), jnp.int32))
    blocks = shards.reshape(-1, ORDERS, shards.shape[2] // height, height, width)
    blocks = jnp.swapaxes(blocks, 1, 2).reshape(rows, ORDERS, height, width)
    return 2.0 * window_tiles - sum_over_row(blocks, rows)


def solution(mesh):
    return jax.shard_map(
        functools.partial(on_device, mesh.shape["col"], mesh.shape["row"]),
        mesh=mesh,
        in_specs=(P(None, "col", "row"), P(None, "row", "col"), P(None, "row", "col")),
        out_specs=P(None, "row", "col"),
        check_vma=False,
    )
```
